256 devices in a mesh: freq: 4 (over x_hi, core), xband: 64 (over y, z, x_lo).
Axes of the slice: x: 4 (x_hi: 2, x_lo: 2; x = x_hi * 2 + x_lo), y: 4, z: 8, core: 2. Of those that a mesh axis runs over, the one named last changes fastest.
Arguments:
- source_field: float32 [8, 2, 1024, 2048], P('freq', None, 'xband'), may hold values from -6 to 6
- receiver_field: float32 [8, 2, 1024, 2048], P('freq', None, 'xband'), may hold values from -6 to 6
- adjoint_field: float32 [8, 2, 1024, 2048], P('freq', None, 'xband'), may hold values from -6 to 6
- slowness: float32 [4, 1024, 2048], P('freq', 'xband'), may hold values from 0.8 to 1.25
- epsilon_field: float32 [4, 1024, 2048], P('freq', 'xband'), may hold values from 0 to 0.25
- delta_field: float32 [4, 1024, 2048], P('freq', 'xband'), may hold values from 0 to 0.25
- depth_slab: int32 [4], replicated, may hold values from 0 to 3, each once
- freq_index: int32 [8], P('freq'), may hold values from 0 to 7, each once
Outputs:
- adjoint_final: float32 [8, 2, 1024, 2048], P('freq', None, 'xband')
- image_stack: float32 [4, 1024, 2048], P(None, 'xband')
- model_gradient: float32 [4, 3, 1024, 2048], P('freq', None, 'xband')
The draws below stay inside these ranges and needn't reach their ends.
Inputs may be any that keep to these rules, and one draw needn't show every extreme that they name: `depth_slab`: each of the 4 slabs is used by exactly one depth step. `freq_index`: each frequency number is held by exactly one slot.
All inputs are finite; a program needn't handle non-finite values.
Results may differ from the reference program's by a relative error of at most 0.0001.
Values sent between devices are 32-bit elements; how exact they have to be, the bound alone decides.
A program may use at most 64 MiB of HBM per device.

```python
import math
import jax
import jax.numpy as jnp

NI = 2048
FREQS = 8
NX = 1024
ZSTEPS = 4


def block_scale(stream_key, extent, pieces, least, top_value):
    factor_of, own = 1.0, jax.random.fold_in(stream_key, 6)
    for position, shards_of in pieces:
        draws = jnp.exp(jax.random.uniform(jax.random.fold_in(own, position), (shards_of,), jnp.float32, least / len(pieces), top_value / len(pieces)))
        factor_of = factor_of * jnp.repeat(draws, extent[position] // shards_of).reshape([-1 if axis == position else 1 for axis in range(len(extent))])
    return factor_of


def normal_values(key, shape, spread, most, pieces=(), dtype=jnp.bfloat16):
    factor_of = block_scale(key, shape, pieces, -0.22, 0.18) if pieces else 1.0
    entries = jax.random.normal(key, shape, jnp.float32) * spread * factor_of
    return jnp.minimum(jnp.maximum(entries, -most), most).astype(dtype)


def setup_inputs(seed: int = 0) -> dict:
    key_of = jax.random.split(jax.random.key(seed), 9)
    source_field = normal_values(key_of[0], (FREQS, 2, NX, NI), 1.0, 6.0, ((0, 4), (2, 64)), jnp.float32)
    receiver_field = normal_values(key_of[1], (FREQS, 2, NX, NI), 1.0, 6.0, ((0, 4), (2, 64)), jnp.float32)
    adjoint_field = normal_values(key_of[2], (FREQS, 2, NX, NI), 1.0, 6.0, ((0, 4), (2, 64)), jnp.float32)
    slowness = jnp.clip(jnp.exp(math.log(1.25) - 0.4462871 * jax.random.uniform(key_of[3], (ZSTEPS, NX, NI), jnp.float32) ** block_scale(key_of[3], (ZSTEPS, NX, NI), ((0, 4), (1, 64)), -0.2, 0.2)), 0.8, 1.25)
    epsilon_field = jnp.clip(0.25 * jax.random.uniform(key_of[4], (ZSTEPS, NX, NI), jnp.float32) ** block_scale(key_of[4], (ZSTEPS, NX, NI), ((0, 4), (1, 64)), -0.2, 0.2), 0.0, 0.25)
    delta_field = jnp.clip(0.25 * jax.random.uniform(key_of[5], (ZSTEPS, NX, NI), jnp.float32) ** block_scale(key_of[5], (ZSTEPS, NX, NI), ((0, 4), (1, 64)), -0.2, 0.2), 0.0, 0.25)
    depth_slab = jax.random.permutation(key_of[6], ZSTEPS).astype(jnp.int32)
    freq_index = jax.random.permutation(key_of[7], FREQS).astype(jnp.int32)
    return {"source_field": source_field, "receiver_field": receiver_field, "adjoint_field": adjoint_field, "slowness": slowness, "epsilon_field": epsilon_field, "delta_field": delta_field, "depth_slab": depth_slab, "freq_index": freq_index}


BASE_FREQ = 2.0
FREQ_STEP = 0.25
DISPERSE = 0.08
DIFFUSE = 0.05
FORCING = 0.5


def laplace(values):
    widths = [(0, 0)] * (values.ndim - 2) + [(1, 1), (1, 1)]
    padded = jnp.pad(values, widths)
    return (padded[..., 2:, 1:-1] + padded[..., :-2, 1:-1] + padded[..., 1:-1, 2:] + padded[..., 1:-1, :-2] - 4.0 * values)


def extrapolate(wavefield, angular, slow_part, eps_part, del_part, sign_value):
    phase_angle = sign_value * angular * (slow_part * (1.0 + eps_part))
    cosine = jnp.cos(phase_angle)
    sine_val = jnp.sin(phase_angle)
    real_part = wavefield[:, 0] * cosine - wavefield[:, 1] * sine_val
    imag_part = wavefield[:, 0] * sine_val + wavefield[:, 1] * cosine
    coupling = sign_value * DISPERSE * (1.0 + 2.0 * del_part) * BASE_FREQ / (angular * slow_part)
    lap_real = laplace(real_part)
    lap_imag = laplace(imag_part)
    new_real = real_part + DIFFUSE * lap_real - coupling * lap_imag
    new_imag = imag_part + DIFFUSE * lap_imag + coupling * lap_real
    return jnp.stack([new_real, new_imag], axis=1)


def reference(source_field, receiver_field, adjoint_field, slowness, epsilon_field, delta_field, depth_slab, freq_index):
    angular = (BASE_FREQ + FREQ_STEP * freq_index.astype(jnp.float32))[:, None, None]
    freq_count = source_field.shape[0]
    gradient = jnp.zeros((slowness.shape[0], 3) + slowness.shape[1:], jnp.float32)
    images = []
    for depth_step in range(ZSTEPS):
        slab_index = depth_slab[depth_step]
        slow_part = slowness[slab_index]
        eps_part = epsilon_field[slab_index]
        del_part = delta_field[slab_index]
        source_field = extrapolate(source_field, angular, slow_part, eps_part, del_part, 1.0)
        receiver_field = extrapolate(receiver_field, angular, slow_part, eps_part, del_part, -1.0)
        moved_adjoint = extrapolate(adjoint_field, angular, slow_part, eps_part, del_part, -1.0)
        image_depth = jnp.sum(source_field[:, 0] * receiver_field[:, 0] + source_field[:, 1] * receiver_field[:, 1], axis=0) / freq_count
        images.append(image_depth)
        adjoint_field = moved_adjoint + FORCING * image_depth * source_field
        slow_term = jnp.sum(angular * (source_field[:, 0] * adjoint_field[:, 1] - source_field[:, 1] * adjoint_field[:, 0]), axis=0)
        aniso_term = jnp.sum(angular * (receiver_field[:, 0] * adjoint_field[:, 1] - receiver_field[:, 1] * adjoint_field[:, 0]), axis=0)
        delta_term = jnp.sum((BASE_FREQ / angular) * (source_field[:, 0] * adjoint_field[:, 0] + source_field[:, 1] * adjoint_field[:, 1]), axis=0)
        grad_terms = jnp.stack([slow_term, aniso_term, delta_term]) / freq_count
        gradient = gradient.at[slab_index].set(grad_terms)
    return adjoint_field, jnp.stack(images), gradient
```

```python
import functools

import jax
import jax.numpy as jnp
from jax import lax
from jax.experimental import pallas as pl
from jax.experimental.pallas import tpu as pltpu
from jax.sharding import PartitionSpec as P

BASE_FREQ = 2.0
FREQ_STEP = 0.25
DISPERSE = 0.08
DIFFUSE = 0.05
FORCING = 0.5
MESH = pl.DeviceIdType.MESH

PI_HI = 3.140625
PI_LO = 9.67653589793e-4
SIN = (
    1.0,
    -0.16666655242443085,
    0.008333146572113037,
    -0.00019830558449029922,
    2.7278699690214125e-06,
    -2.1673399075439193e-08,
)
COS = (
    1.0,
    -0.4999999701976776,
    0.04166661947965622,
    -0.0013888514367863536,
    2.478722672094591e-05,
    -2.7273267733107787e-07,
    1.805915972319383e-09,
)

STEPS = 4
NF = 4
ROWS = 8
SLABS = 4


def horner(coefs, x):
    total = coefs[-1] * x + coefs[-2]
    for coef in coefs[-3::-1]:
        total = total * x + coef
    return total


def cos_sin(phase):
    t = (phase - PI_HI) - PI_LO
    t2 = t * t
    return -horner(COS, t2), -(t * horner(SIN, t2))


def kernel(
    bands,
    src_hbm,
    rec_hbm,
    adj_hbm,
    slow_hbm,
    eps_hbm,
    del_hbm,
    slab_ref,
    fidx_ref,
    adj_out,
    img_out,
    grad_out,
    sed,
    model,
    msend,
    angb,
    first,
    sr,
    vsr,
    va,
    adj,
    cs,
    row_sr,
    halo_sr,
    row_a,
    halo_a,
    ipart,
    irecv,
    img,
    grad,
    gsend,
    grecv,
    gfin,
    gown,
    gsib,
    local_sem,
    send_sem,
    recv_sem,
):
    ni = sed.shape[-1]
    f = lax.axis_index("freq")
    b = lax.axis_index("xband")
    c = lax.rem(f, 2)
    o = 1 - c
    sib_f = f + 1 - 2 * c
    sib = (sib_f, b)
    far = (lax.rem(f + 2, 4), b)
    farx = (lax.rem(sib_f + 2, 4), b)
    neighbour = (sib_f, lax.rem(b + 2 * c - 1 + bands, bands))

    counts = {"local": 0, "remote": 0}

    def local_copy(source, target):
        k = counts["local"]
        counts["local"] += 1
        copy = pltpu.make_async_copy(source, target, local_sem.at[k])
        copy.start()
        return copy

    def remote_copy(source, target, device):
        k = counts["remote"]
        counts["remote"] += 1
        copy = pltpu.make_async_remote_copy(
            src_ref=source,
            dst_ref=target,
            send_sem=send_sem.at[k],
            recv_sem=recv_sem.at[k],
            device_id=device,
            device_id_type=MESH,
        )
        copy.start()
        return copy

    mine = pl.ds(pl.multiple_of(c * ROWS, ROWS), ROWS)
    theirs = pl.ds(pl.multiple_of(o * ROWS, ROWS), ROWS)
    my_slots = pl.ds(2 * c, 2)
    their_slots = pl.ds(2 * o, 2)

    barrier = pltpu.get_barrier_semaphore()
    for device in (sib, far, farx, neighbour):
        pl.semaphore_signal(barrier, inc=1, device_id=device, device_id_type=MESH)

    loads = [
        local_copy(ref.at[0], sed.at[k]) for k, ref in enumerate((slow_hbm, eps_hbm, del_hbm))
    ]
    fields_hbm = (src_hbm, rec_hbm, adj_hbm)
    own_fields = [
        local_copy(ref.at[:, :, mine], first.at[k, my_slots]) for k, ref in enumerate(fields_hbm)
    ]

    for k in range(2):
        value = BASE_FREQ + FREQ_STEP * fidx_ref[k].astype(jnp.float32)
        angb[2 * c + k] = jnp.full((8, 128), value, jnp.float32)

    for copy in loads:
        copy.wait()
    for rows, ref in ((mine, model.at[f]), (theirs, msend)):
        slow = sed[0, rows]
        ref[0] = slow * (1.0 + sed[1, rows])
        ref[1] = (1.0 + 2.0 * sed[2, rows]) / slow

    pl.semaphore_wait(barrier, 4)
    sends = []
    models = [
        remote_copy(model.at[f], model.at[f], far),
        remote_copy(msend, model.at[f], farx),
        remote_copy(msend, model.at[f], sib),
    ]
    angs = remote_copy(angb.at[my_slots], angb.at[my_slots], sib)
    fields = [
        remote_copy(ref.at[:, :, theirs], first.at[k, my_slots], sib)
        for k, ref in enumerate(fields_hbm)
    ]
    sends += models + [angs] + fields
    for copy in [angs] + models:
        copy.wait_recv()

    slabs = [slab_ref[z] for z in range(STEPS)]
    lanes = lax.broadcasted_iota(jnp.int32, (ROWS, 128), 1)
    sublanes = lax.broadcasted_iota(jnp.int32, (ROWS, ni), 0)
    top_row = sublanes == 0
    last_row = sublanes == ROWS - 1
    keep_top = jnp.where((c == 0) & (b == 0), 0.0, 1.0)
    keep_last = jnp.where((c == 1) & (b == bands - 1), 0.0, 1.0)

    def wide(tile):
        return jnp.concatenate([tile] * (ni // 128), axis=1)

    def trig(z):
        def body(k, carry):
            cosine, sine = cos_sin(wide(angb[k]) * model[slabs[z], 0])
            cs[z, k, 0] = cosine
            cs[z, k, 1] = sine
            return carry

        lax.fori_loop(0, NF, body, 0)

    def rotate(p, q, cosine, sine, sign):
        if sign > 0:
            return p * cosine - q * sine, p * sine + q * cosine
        return p * cosine + q * sine, q * cosine - p * sine

    def put_rows(rows, z, k, j, value):
        rows[z, 0, k, pl.ds(j, 1), :] = value[0:1, :]
        rows[z, 1, k, pl.ds(j, 1), :] = value[ROWS - 1 : ROWS, :]

    def around(v, halos, z, k, j):
        top = halos[z, 0, k, pl.ds(j, 1), :] * keep_top
        last = halos[z, 1, k, pl.ds(j, 1), :] * keep_last
        above = jnp.where(top_row, top, pltpu.roll(v, 1, 0))
        below = jnp.where(last_row, last, pltpu.roll(v, ROWS - 1, 0))
        before = pltpu.roll(v, 1, 1)
        before = jnp.concatenate(
            [jnp.where(lanes == 0, 0.0, before[:, :128]), before[:, 128:]], axis=1
        )
        after = pltpu.roll(v, ni - 1, 1)
        after = jnp.concatenate(
            [after[:, :-128], jnp.where(lanes == 127, 0.0, after[:, -128:])], axis=1
        )
        return (above + below) + (before + after)

    def spread(vr, vi, halos, z, k, j, coupling):
        lap_r = around(vr, halos, z, k, j) - 4.0 * vr
        lap_i = around(vi, halos, z, k, j + 1) - 4.0 * vi
        return (
            vr + DIFFUSE * lap_r - coupling * lap_i,
            vi + DIFFUSE * lap_i + coupling * lap_r,
        )

    def couple(z, k):
        return wide(DISPERSE * BASE_FREQ / angb[k]) * model[slabs[z], 1]

    def rotate_sr(z, k, values):
        cosine, sine = cs[z, k, 0], cs[z, k, 1]
        rotated = rotate(values[0], values[1], cosine, sine, 1) + rotate(
            values[2], values[3], cosine, sine, -1
        )
        for j, value in enumerate(rotated):
            vsr[k, j] = value
            put_rows(row_sr, z, k, j, value)

    def rotate_a(z, k, real, imag):
        rotated = rotate(real, imag, cs[z, k, 0], cs[z, k, 1], -1)
        for j, value in enumerate(rotated):
            va[k, j] = value
            put_rows(row_a, z, k, j, value)

    def send_rows(rows, halos, z):
        return [
            remote_copy(rows.at[z, c], halos.at[z, o], neighbour),
            remote_copy(rows.at[z, o], halos.at[z, c], sib),
        ]

    def first_sr(k, carry):
        rotate_sr(0, k, (first[0, k, 0], first[0, k, 1], first[1, k, 0], first[1, k, 1]))
        return carry

    def first_a(k, carry):
        rotate_a(0, k, first[2, k, 0], first[2, k, 1])
        return carry

    def pass_sr(z):
        def body(k, total):
            coupling = couple(z, k)
            s_r, s_i = spread(vsr[k, 0], vsr[k, 1], halo_sr, z, k, 0, coupling)
            r_r, r_i = spread(vsr[k, 2], vsr[k, 3], halo_sr, z, k, 2, -coupling)
            for j, value in enumerate((s_r, s_i, r_r, r_i)):
                sr[z, k, j] = value
            if z + 1 < STEPS:
                rotate_sr(z + 1, k, (s_r, s_i, r_r, r_i))
            return total + (s_r * r_r + s_i * r_i)

        ipart[z] = lax.fori_loop(0, NF, body, jnp.zeros((ROWS, ni), jnp.float32))

    def pass_a(z):
        def body(k, carry):
            a_r, a_i = spread(va[k, 0], va[k, 1], halo_a, z, k, 0, -couple(z, k))
            adj[k, 0] = a_r
            adj[k, 1] = a_i
            return carry

        lax.fori_loop(0, NF, body, 0)

    def force(z):
        def body(k, totals):
            ang = wide(angb[k])
            inv = wide(BASE_FREQ / angb[k])
            s_r, s_i, r_r, r_i = (sr[z, k, j] for j in range(4))
            half = FORCING * img[z]
            a_r = adj[k, 0] + half * s_r
            a_i = adj[k, 1] + half * s_i
            if z + 1 < STEPS:
                rotate_a(z + 1, k, a_r, a_i)
            else:
                adj[k, 0] = a_r
                adj[k, 1] = a_i
            grad[z, 0] = jnp.where(k == 0, 0.0, grad[z, 0]) + ang * (s_r * a_i - s_i * a_r)
            grad[z, 1] = jnp.where(k == 0, 0.0, grad[z, 1]) + ang * (r_r * a_i - r_i * a_r)
            grad[z, 2] = jnp.where(k == 0, 0.0, grad[z, 2]) + inv * (s_r * a_r + s_i * a_i)
            return totals

        lax.fori_loop(0, NF, body, 0)

    trig(0)
    for copy in own_fields[:2]:
        copy.wait()
    for copy in fields[:2]:
        copy.wait_recv()
    lax.fori_loop(0, NF, first_sr, 0)
    wait_sr = send_rows(row_sr, halo_sr, 0)
    own_fields[2].wait()
    fields[2].wait_recv()
    lax.fori_loop(0, NF, first_a, 0)
    wait_a = send_rows(row_a, halo_a, 0)
    sends += wait_sr + wait_a
    trig(1)

    def uses(chip):
        at = []
        for j in range(2):
            step = 0
            for z in range(1, STEPS):
                step = jnp.where(slabs[z] == 2 * chip + j, z, step)
            at.append(step)
        return jnp.minimum(at[0], at[1]), jnp.maximum(at[0], at[1]), at[0] < at[1]

    chip = f // 2
    far_uses = uses(1 - chip)
    my_uses = uses(chip)
    copies = []
    arrivals = []
    gradients = []

    for z in range(STEPS):
        for copy in wait_sr:
            copy.wait_recv()
        pass_sr(z)
        if z + 1 < STEPS:
            wait_sr = send_rows(row_sr, halo_sr, z + 1)
            sends += wait_sr
        image = remote_copy(ipart.at[z], irecv.at[z], far)
        sends.append(image)
        if z + 2 < STEPS:
            trig(z + 2)
        for copy in wait_a:
            copy.wait_recv()
        pass_a(z)
        image.wait_recv()
        img[z] = (ipart[z] + irecv[z]) * (1.0 / (2 * NF))
        force(z)
        if z + 1 < STEPS:
            wait_a = send_rows(row_a, halo_a, z + 1)
            sends += wait_a
        else:
            arrivals.append(remote_copy(adj.at[their_slots], adj_out.at[:, :, mine], sib))
            copies.append(local_copy(adj.at[my_slots], adj_out.at[:, :, mine]))
        if z >= STEPS - 2:
            n = z - (STEPS - 2)
            for j in range(3):
                gsend[n, j] = grad[far_uses[n], j]
            gradients.append(remote_copy(gsend.at[n], grecv.at[n], far))
        copies.append(local_copy(img.at[z], img_out.at[z, mine]))
        arrivals.append(remote_copy(img.at[z], img_out.at[z, mine], sib))
    sends += gradients

    for n in range(2):
        gradients[n].wait_recv()
        for j in range(3):
            gfin[n, j] = (grad[my_uses[n], j] + grecv[n, j]) * (1.0 / (2 * NF))
    first_is_zero = my_uses[2].astype(jnp.int32)
    own_is = jnp.where(c == 0, 1 - first_is_zero, first_is_zero)
    for j in range(3):
        gsib[j] = gfin[1 - own_is, j]
    arrivals.append(remote_copy(gsib, grad_out.at[0, :, mine], sib))
    for j in range(3):
        gown[j] = gfin[own_is, j]
    copies.append(local_copy(gown, grad_out.at[0, :, mine]))
    for copy in arrivals:
        copy.wait_recv()
    for copy in copies:
        copy.wait()
    for copy in sends + arrivals:
        copy.wait_send()


def solution(mesh):
    bands = mesh.shape["xband"]

    def step(*args):
        ni = args[0].shape[-1]
        half = (ROWS, ni)
        f32 = jnp.float32

        def vmem(*shape):
            return pltpu.VMEM(shape, f32)

        scratch = [
            vmem(3, 2 * ROWS, ni),
            vmem(SLABS, 2, *half),
            vmem(2, *half),
            vmem(NF, 8, 128),
            vmem(3, NF, 2, *half),
            vmem(STEPS, NF, 4, *half),
            vmem(NF, 4, *half),
            vmem(NF, 2, *half),
            vmem(NF, 2, *half),
            vmem(STEPS, NF, 2, *half),
            vmem(STEPS, 2, NF, 4, ni),
            vmem(STEPS, 2, NF, 4, ni),
            vmem(STEPS, 2, NF, 2, ni),
            vmem(STEPS, 2, NF, 2, ni),
            vmem(STEPS, *half),
            vmem(STEPS, *half),
            vmem(STEPS, *half),
            vmem(STEPS, 3, *half),
            vmem(2, 3, *half),
            vmem(2, 3, *half),
            vmem(2, 3, *half),
            vmem(3, *half),
            vmem(3, *half),
            pltpu.SemaphoreType.DMA((16,)),
            pltpu.SemaphoreType.DMA((40,)),
            pltpu.SemaphoreType.DMA((40,)),
        ]
        any_spec = pl.BlockSpec(memory_space=pl.ANY)
        smem_spec = pl.BlockSpec(memory_space=pltpu.SMEM)
        return pl.pallas_call(
            functools.partial(kernel, bands),
            out_shape=(
                jax.ShapeDtypeStruct(args[2].shape, f32),
                jax.ShapeDtypeStruct((STEPS,) + args[3].shape[1:], f32),
                jax.ShapeDtypeStruct((1, 3) + args[3].shape[1:], f32),
            ),
            in_specs=[any_spec] * 6 + [smem_spec] * 2,
            out_specs=(any_spec,) * 3,
            scratch_shapes=scratch,
            compiler_params=pltpu.CompilerParams(
                collective_id=0, has_side_effects=True, vmem_limit_bytes=40 * 2**20
            ),
        )(*args)

    return jax.shard_map(
        step,
        mesh=mesh,
        in_specs=(
            P("freq", None, "xband", None),
            P("freq", None, "xband", None),
            P("freq", None, "xband", None),
            P("freq", "xband", None),
            P("freq", "xband", None),
            P("freq", "xband", None),
            P(),
            P("freq"),
        ),
        out_specs=(
            P("freq", None, "xband", None),
            P(None, "xband", None),
            P("freq", None, "xband", None),
        ),
        check_vma=False,
    )
```

```python
import functools

import jax
import jax.numpy as jnp
from jax import lax
from jax.experimental import pallas as pl
from jax.experimental.pallas import tpu as pltpu
from jax.sharding import PartitionSpec as P

BASE_FREQ = 2.0
FREQ_STEP = 0.25
DISPERSE = 0.08
DIFFUSE = 0.05
FORCING = 0.5
MESH = pl.DeviceIdType.MESH

PI_HI = 3.140625
PI_LO = 9.67653589793e-4
SIN = (
    1.0,
    -0.16666655242443085,
    0.008333146572113037,
    -0.00019830558449029922,
    2.7278699690214125e-06,
    -2.1673399075439193e-08,
)
COS = (
    1.0,
    -0.4999999701976776,
    0.04166661947965622,
    -0.0013888514367863536,
    2.478722672094591e-05,
    -2.7273267733107787e-07,
    1.805915972319383e-09,
)

STEPS = 4
NF = 4
ROWS = 8
SLABS = 4
LAG = 1


def horner(coefs, x):
    total = coefs[-1] * x + coefs[-2]
    for coef in coefs[-3::-1]:
        total = total * x + coef
    return total


def cos_sin(phase):
    t = (phase - PI_HI) - PI_LO
    t2 = t * t
    return -horner(COS, t2), -(t * horner(SIN, t2))


def kernel(
    bands,
    src_hbm,
    rec_hbm,
    adj_hbm,
    slow_hbm,
    eps_hbm,
    del_hbm,
    slab_hbm,
    fidx_hbm,
    adj_out,
    img_out,
    grad_out,
    sed,
    model,
    msend,
    angb,
    first,
    sr,
    vsr,
    va,
    adj,
    cs,
    row_sr,
    halo_sr,
    row_a,
    halo_a,
    ipart,
    irecv,
    img,
    grad,
    gsend,
    grecv,
    gfin,
    gown,
    gsib,
    slab_ref,
    fidx_ref,
    stage,
    edge_send,
    edge_recv,
    slow_send,
    slow_recv,
    local_sem,
    send_sem,
    recv_sem,
    sr_send_sem,
    sr_recv_sem,
    edge_send_sem,
    edge_recv_sem,
    slow_send_sem,
    slow_recv_sem,
):
    ni = sed.shape[-1]
    f = lax.axis_index("freq")
    b = lax.axis_index("xband")
    c = lax.rem(f, 2)
    o = 1 - c
    sib_f = f + 1 - 2 * c
    sib = (sib_f, b)
    far = (lax.rem(f + 2, 4), b)
    farx = (lax.rem(sib_f + 2, 4), b)
    neighbour = (sib_f, lax.rem(b + 2 * c - 1 + bands, bands))

    counts = {"local": 0, "remote": 0}

    def local_copy(source, target):
        k = counts["local"]
        counts["local"] += 1
        copy = pltpu.make_async_copy(source, target, local_sem.at[k])
        copy.start()
        return copy

    def remote_copy(source, target, device):
        k = counts["remote"]
        counts["remote"] += 1
        copy = pltpu.make_async_remote_copy(
            src_ref=source,
            dst_ref=target,
            send_sem=send_sem.at[k],
            recv_sem=recv_sem.at[k],
            device_id=device,
            device_id_type=MESH,
        )
        copy.start()
        return copy

    mine = pl.ds(pl.multiple_of(c * ROWS, ROWS), ROWS)
    theirs = pl.ds(pl.multiple_of(o * ROWS, ROWS), ROWS)
    my_slots = pl.ds(2 * c, 2)
    their_slots = pl.ds(2 * o, 2)

    outer_band = lax.rem(b + 2 * c - 1 + bands, bands)
    after_band = lax.rem(b + 1, bands)
    before_band = lax.rem(b + bands - 1, bands)
    chip = f // 2
    barrier = pltpu.get_barrier_semaphore()
    for device in [sib, far, farx] + [(k, outer_band) for k in range(4)]:
        pl.semaphore_signal(barrier, inc=1, device_id=device, device_id_type=MESH)

    ints = [local_copy(fidx_hbm, fidx_ref), local_copy(slab_hbm, slab_ref)]
    loads = [
        local_copy(ref.at[0], sed.at[k]) for k, ref in enumerate((slow_hbm, eps_hbm, del_hbm))
    ]
    fields_hbm = (src_hbm, rec_hbm, adj_hbm)
    stages = [local_copy(ref, stage.at[k]) for k, ref in enumerate(fields_hbm[:2])]
    own_fields = [
        local_copy(ref.at[:, :, mine], first.at[k, my_slots]) for k, ref in enumerate(fields_hbm)
    ]

    ints[0].wait()
    for k in range(2):
        value = BASE_FREQ + FREQ_STEP * fidx_ref[k].astype(jnp.float32)
        angb[2 * c + k] = jnp.full((8, 128), value, jnp.float32)

    for copy in loads:
        copy.wait()
    for rows, ref in ((mine, model.at[f]), (theirs, msend)):
        slow = sed[0, rows]
        ref[0] = slow * (1.0 + sed[1, rows])
        ref[1] = (1.0 + 2.0 * sed[2, rows]) / slow
    for side, row in ((0, 0), (1, 2 * ROWS - 1)):
        slow_send[side] = sed[0, row : row + 1] * (1.0 + sed[1, row : row + 1])
    def edge_copy(side, sender, device):
        return pltpu.make_async_remote_copy(
            src_ref=edge_send.at[side],
            dst_ref=edge_recv.at[sender],
            send_sem=edge_send_sem.at[side],
            recv_sem=edge_recv_sem.at[sender],
            device_id=device,
            device_id_type=MESH,
        )

    def slow_copy(n, sender, device):
        return pltpu.make_async_remote_copy(
            src_ref=slow_send.at[n // 2],
            dst_ref=slow_recv.at[sender],
            send_sem=slow_send_sem.at[n],
            recv_sem=slow_recv_sem.at[sender],
            device_id=device,
            device_id_type=MESH,
        )

    pl.semaphore_wait(barrier, 7)
    sends = []
    models = [
        remote_copy(model.at[f], model.at[f], far),
        remote_copy(msend, model.at[f], farx),
        remote_copy(msend, model.at[f], sib),
    ]
    early = [
        edge_copy(0, c, (2 * chip + 1, before_band)),
        edge_copy(1, c, (2 * chip, after_band)),
        slow_copy(0, f, (1, before_band)),
        slow_copy(1, f, (3, before_band)),
        slow_copy(2, f, (0, after_band)),
        slow_copy(3, f, (2, after_band)),
    ]
    for copy in early[2:]:
        copy.start()
    for copy in stages:
        copy.wait()
    for side, row in ((0, 0), (1, 2 * ROWS - 1)):
        for field in range(2):
            for k in range(2):
                for part in range(2):
                    at = 2 * field + k
                    edge_send[side, part, at : at + 1] = stage[field, k, part, row : row + 1]

    for copy in early[:2]:
        copy.start()
    angs = remote_copy(angb.at[my_slots], angb.at[my_slots], sib)
    fields = [
        remote_copy(ref.at[:, :, theirs], first.at[k, my_slots], sib)
        for k, ref in enumerate(fields_hbm)
    ]
    sends += models + [angs] + fields + early
    for copy in [angs] + models:
        copy.wait_recv()

    ints[1].wait()
    slabs = [slab_ref[z] for z in range(STEPS)]
    lanes = lax.broadcasted_iota(jnp.int32, (ROWS, 128), 1)
    sublanes = lax.broadcasted_iota(jnp.int32, (ROWS, ni), 0)
    top_row = sublanes == 0
    last_row = sublanes == ROWS - 1
    keep_top = jnp.where((c == 0) & (b == 0), 0.0, 1.0)
    keep_last = jnp.where((c == 1) & (b == bands - 1), 0.0, 1.0)

    def wide(tile):
        return jnp.concatenate([tile] * (ni // 128), axis=1)

    def trig(z):
        def body(k, carry):
            cosine, sine = cos_sin(wide(angb[k]) * model[slabs[z], 0])
            cs[z, k, 0] = cosine
            cs[z, k, 1] = sine
            return carry

        lax.fori_loop(0, NF, body, 0)

    def rotate(p, q, cosine, sine, sign):
        if sign > 0:
            return p * cosine - q * sine, p * sine + q * cosine
        return p * cosine + q * sine, q * cosine - p * sine

    def put_rows(rows, z, k, j, value):
        rows[z, 0, k, pl.ds(j, 1), :] = value[0:1, :]
        rows[z, 1, k, pl.ds(j, 1), :] = value[ROWS - 1 : ROWS, :]

    def around(v, halos, z, k, j):
        top = halos[z, 0, k, pl.ds(j, 1), :] * keep_top
        last = halos[z, 1, k, pl.ds(j, 1), :] * keep_last
        above = jnp.where(top_row, top, pltpu.roll(v, 1, 0))
        below = jnp.where(last_row, last, pltpu.roll(v, ROWS - 1, 0))
        before = pltpu.roll(v, 1, 1)
        before = jnp.concatenate(
            [jnp.where(lanes == 0, 0.0, before[:, :128]), before[:, 128:]], axis=1
        )
        after = pltpu.roll(v, ni - 1, 1)
        after = jnp.concatenate(
            [after[:, :-128], jnp.where(lanes == 127, 0.0, after[:, -128:])], axis=1
        )
        return (above + below) + (before + after)

    def spread(vr, vi, halos, z, k, j, coupling):
        lap_r = around(vr, halos, z, k, j) - 4.0 * vr
        lap_i = around(vi, halos, z, k, j + 1) - 4.0 * vi
        return (
            vr + DIFFUSE * lap_r - coupling * lap_i,
            vi + DIFFUSE * lap_i + coupling * lap_r,
        )

    def couple(z, k):
        return wide(DISPERSE * BASE_FREQ / angb[k]) * model[slabs[z], 1]

    def rotate_sr(z, k, values):
        cosine, sine = cs[z, k, 0], cs[z, k, 1]
        rotated = rotate(values[0], values[1], cosine, sine, 1) + rotate(
            values[2], values[3], cosine, sine, -1
        )
        for j, value in enumerate(rotated):
            vsr[k, j] = value
            put_rows(row_sr, z, k, j, value)

    def rotate_a(z, k, real, imag):
        rotated = rotate(real, imag, cs[z, k, 0], cs[z, k, 1], -1)
        for j, value in enumerate(rotated):
            va[k, j] = value
            put_rows(row_a, z, k, j, value)

    def send_rows(rows, halos, z):
        return [
            remote_copy(rows.at[z, c], halos.at[z, o], neighbour),
            remote_copy(rows.at[z, o], halos.at[z, c], sib),
        ]

    def sr_outer(z, k):
        return pltpu.make_async_remote_copy(
            src_ref=row_sr.at[z, c, k],
            dst_ref=halo_sr.at[z, o, k],
            send_sem=sr_send_sem.at[z, k, 0],
            recv_sem=sr_recv_sem.at[z, k, 0],
            device_id=neighbour,
            device_id_type=MESH,
        )

    def sr_inner(z, k):
        return pltpu.make_async_remote_copy(
            src_ref=row_sr.at[z, o, k],
            dst_ref=halo_sr.at[z, c, k],
            send_sem=sr_send_sem.at[z, k, 1],
            recv_sem=sr_recv_sem.at[z, k, 1],
            device_id=sib,
            device_id_type=MESH,
        )

    def first_edges():
        slow_row = slow_recv[slabs[0]]
        rows4 = lax.broadcasted_iota(jnp.int32, (4, ni), 0)
        for core in range(2):
            tile = jnp.where(
                lax.broadcasted_iota(jnp.int32, (4, 128), 0) % 2 == 0,
                angb[2 * core, 0:4],
                angb[2 * core + 1, 0:4],
            )
            cosine, sine = cos_sin(wide(tile) * slow_row)
            sine = jnp.where(rows4 < 2, sine, -sine)
            p, q = edge_recv[core, 0], edge_recv[core, 1]
            real, imag = p * cosine - q * sine, p * sine + q * cosine
            for field in range(2):
                for k in range(2):
                    at = 2 * field + k
                    halo_sr[0, c, 2 * core + k, 2 * field : 2 * field + 1] = real[at : at + 1]
                    halo_sr[0, c, 2 * core + k, 2 * field + 1 : 2 * field + 2] = imag[at : at + 1]

    def first_sr(k, carry):
        rotate_sr(0, k, (first[0, k, 0], first[0, k, 1], first[1, k, 0], first[1, k, 1]))
        sr_inner(0, k).start()
        return carry

    def first_a(k, carry):
        rotate_a(0, k, first[2, k, 0], first[2, k, 1])
        return carry

    def pass_sr(z):
        def body(k, total):
            coupling = couple(z, k)
            if z > 0:
                sr_outer(z, k).wait_recv()
            sr_inner(z, k).wait_recv()
            s_r, s_i = spread(vsr[k, 0], vsr[k, 1], halo_sr, z, k, 0, coupling)
            r_r, r_i = spread(vsr[k, 2], vsr[k, 3], halo_sr, z, k, 2, -coupling)
            for j, value in enumerate((s_r, s_i, r_r, r_i)):
                sr[z, k, j] = value
            if z + 1 < STEPS:
                rotate_sr(z + 1, k, (s_r, s_i, r_r, r_i))
                sr_outer(z + 1, k).start()
                sr_inner(z + 1, k).start()
            return total + (s_r * r_r + s_i * r_i)

        ipart[z] = lax.fori_loop(0, NF, body, jnp.zeros((ROWS, ni), jnp.float32))

    def pass_a(z):
        def body(k, carry):
            a_r, a_i = spread(va[k, 0], va[k, 1], halo_a, z, k, 0, -couple(z, k))
            adj[k, 0] = a_r
            adj[k, 1] = a_i
            return carry

        lax.fori_loop(0, NF, body, 0)

    def force(z):
        def body(k, totals):
            ang = wide(angb[k])
            inv = wide(BASE_FREQ / angb[k])
            s_r, s_i, r_r, r_i = (sr[z, k, j] for j in range(4))
            half = FORCING * img[z]
            a_r = adj[k, 0] + half * s_r
            a_i = adj[k, 1] + half * s_i
            if z + 1 < STEPS:
                rotate_a(z + 1, k, a_r, a_i)
            else:
                adj[k, 0] = a_r
                adj[k, 1] = a_i
            grad[z, 0] = jnp.where(k == 0, 0.0, grad[z, 0]) + ang * (s_r * a_i - s_i * a_r)
            grad[z, 1] = jnp.where(k == 0, 0.0, grad[z, 1]) + ang * (r_r * a_i - r_i * a_r)
            grad[z, 2] = jnp.where(k == 0, 0.0, grad[z, 2]) + inv * (s_r * a_r + s_i * a_i)
            return totals

        lax.fori_loop(0, NF, body, 0)

    trig(0)
    for copy in own_fields[:2]:
        copy.wait()
    for copy in fields[:2]:
        copy.wait_recv()
    lax.fori_loop(0, NF, first_sr, 0)
    for core in range(2):
        edge_copy(0, core, sib).wait_recv()
    for k in range(SLABS):
        slow_copy(0, k, sib).wait_recv()
    first_edges()
    trig(1)

    def uses(chip):
        at = []
        for j in range(2):
            step = 0
            for z in range(1, STEPS):
                step = jnp.where(slabs[z] == 2 * chip + j, z, step)
            at.append(step)
        return jnp.minimum(at[0], at[1]), jnp.maximum(at[0], at[1]), at[0] < at[1]

    far_uses = uses(1 - chip)
    my_uses = uses(chip)
    copies = []
    arrivals = []
    gradients = []

    def finish(z, wait_a, image):
        for copy in wait_a:
            copy.wait_recv()
        pass_a(z)
        image.wait_recv()
        img[z] = (ipart[z] + irecv[z]) * (1.0 / (2 * NF))
        force(z)
        wait_a = []
        if z + 1 < STEPS:
            wait_a = send_rows(row_a, halo_a, z + 1)
            sends.extend(wait_a)
        if z >= STEPS - 2:
            n = z - (STEPS - 2)
            for j in range(3):
                gsend[n, j] = grad[far_uses[n], j]
                gradients.append(remote_copy(gsend.at[n, j], grecv.at[n, j], far))
        if z + 1 == STEPS:
            arrivals.append(remote_copy(adj.at[their_slots], adj_out.at[:, :, mine], sib))
            copies.append(local_copy(adj.at[my_slots], adj_out.at[:, :, mine]))
        copies.append(local_copy(img.at[z], img_out.at[z, mine]))
        arrivals.append(remote_copy(img.at[z], img_out.at[z, mine], sib))
        return wait_a

    images = []
    for z in range(STEPS):
        pass_sr(z)
        images.append(remote_copy(ipart.at[z], irecv.at[z], far))
        if z == 0:
            own_fields[2].wait()
            fields[2].wait_recv()
            lax.fori_loop(0, NF, first_a, 0)
            wait_a = send_rows(row_a, halo_a, 0)
            sends += wait_a
        if z + 2 < STEPS:
            trig(z + 2)
        if LAG == 0:
            wait_a = finish(z, wait_a, images[z])
        elif z > 0:
            wait_a = finish(z - 1, wait_a, images[z - 1])
    if LAG:
        wait_a = finish(STEPS - 1, wait_a, images[STEPS - 1])
    sends += images
    sends += gradients

    first_is_zero = my_uses[2].astype(jnp.int32)
    own_is = jnp.where(c == 0, 1 - first_is_zero, first_is_zero)
    for j in range(3):
        for n in range(2):
            gradients[3 * n + j].wait_recv()
            gfin[n, j] = (grad[my_uses[n], j] + grecv[n, j]) * (1.0 / (2 * NF))
        gsib[j] = gfin[1 - own_is, j]
        arrivals.append(remote_copy(gsib.at[j], grad_out.at[0, j, mine], sib))
        gown[j] = gfin[own_is, j]
        copies.append(local_copy(gown.at[j], grad_out.at[0, j, mine]))
    for copy in arrivals:
        copy.wait_recv()
    for copy in copies:
        copy.wait()
    for copy in sends + arrivals:
        copy.wait_send()
    for z in range(STEPS):
        for k in range(NF):
            if z > 0:
                sr_outer(z, k).wait_send()
            sr_inner(z, k).wait_send()


def hand_over(*refs):
    copies = [
        pltpu.make_async_copy(refs[k], refs[3 + k], refs[6].at[k]) for k in range(3)
    ]
    for copy in copies:
        copy.start()
    for copy in copies:
        copy.wait()


def solution(mesh):
    bands = mesh.shape["xband"]

    def step(*args):
        args = [pltpu.with_memory_space_constraint(x, pltpu.HBM) for x in args]
        ni = args[0].shape[-1]
        half = (ROWS, ni)
        f32 = jnp.float32

        def vmem(*shape):
            return pltpu.VMEM(shape, f32)

        scratch = [
            vmem(3, 2 * ROWS, ni),
            vmem(SLABS, 2, *half),
            vmem(2, *half),
            vmem(NF, 8, 128),
            vmem(3, NF, 2, *half),
            vmem(STEPS, NF, 4, *half),
            vmem(NF, 4, *half),
            vmem(NF, 2, *half),
            vmem(NF, 2, *half),
            vmem(STEPS, NF, 2, *half),
            vmem(STEPS, 2, NF, 4, ni),
            vmem(STEPS, 2, NF, 4, ni),
            vmem(STEPS, 2, NF, 2, ni),
            vmem(STEPS, 2, NF, 2, ni),
            vmem(STEPS, *half),
            vmem(STEPS, *half),
            vmem(STEPS, *half),
            vmem(STEPS, 3, *half),
            vmem(2, 3, *half),
            vmem(2, 3, *half),
            vmem(2, 3, *half),
            vmem(3, *half),
            vmem(3, *half),
            pltpu.SMEM(args[6].shape, jnp.int32),
            pltpu.SMEM(args[7].shape, jnp.int32),
            vmem(2, 2, 2, 2 * ROWS, ni),
            vmem(2, 2, 4, ni),
            vmem(2, 2, 4, ni),
            vmem(2, 1, ni),
            vmem(SLABS, 1, ni),
            pltpu.SemaphoreType.DMA((24,)),
            pltpu.SemaphoreType.DMA((40,)),
            pltpu.SemaphoreType.DMA((40,)),
            pltpu.SemaphoreType.DMA((STEPS, NF, 2)),
            pltpu.SemaphoreType.DMA((STEPS, NF, 2)),
            pltpu.SemaphoreType.DMA((2,)),
            pltpu.SemaphoreType.DMA((2,)),
            pltpu.SemaphoreType.DMA((4,)),
            pltpu.SemaphoreType.DMA((SLABS,)),
        ]
        any_spec = pl.BlockSpec(memory_space=pl.ANY)
        hbm_spec = pl.BlockSpec(memory_space=pltpu.HBM)
        outs = pl.pallas_call(
            functools.partial(kernel, bands),
            out_shape=(
                jax.ShapeDtypeStruct(args[2].shape, f32),
                jax.ShapeDtypeStruct((STEPS,) + args[3].shape[1:], f32),
                jax.ShapeDtypeStruct((1, 3) + args[3].shape[1:], f32),
            ),
            in_specs=[hbm_spec] * 8,
            out_specs=(any_spec,) * 3,
            scratch_shapes=scratch,
            compiler_params=pltpu.CompilerParams(
                collective_id=0, has_side_effects=True, vmem_limit_bytes=40 * 2**20
            ),
        )(*args)
        return pl.pallas_call(
            hand_over,
            out_shape=tuple(jax.ShapeDtypeStruct(x.shape, f32) for x in outs),
            in_specs=[any_spec] * 3,
            out_specs=(any_spec,) * 3,
            scratch_shapes=[pltpu.SemaphoreType.DMA((3,))],
            compiler_params=pltpu.CompilerParams(vmem_limit_bytes=4 * 2**20),
        )(*outs)

    return jax.shard_map(
        step,
        mesh=mesh,
        in_specs=(
            P("freq", None, "xband", None),
            P("freq", None, "xband", None),
            P("freq", None, "xband", None),
            P("freq", "xband", None),
            P("freq", "xband", None),
            P("freq", "xband", None),
            P(),
            P("freq"),
        ),
        out_specs=(
            P("freq", None, "xband", None),
            P(None, "xband", None),
            P("freq", None, "xband", None),
        ),
        check_vma=False,
    )
```

```python
import functools

import jax
import jax.numpy as jnp
from jax import lax
from jax.experimental import pallas as pl
from jax.experimental.pallas import tpu as pltpu
from jax.sharding import PartitionSpec as P

BASE_FREQ = 2.0
FREQ_STEP = 0.25
DISPERSE = 0.08
DIFFUSE = 0.05
FORCING = 0.5
MESH = pl.DeviceIdType.MESH

PI_HI = 3.140625
PI_LO = 9.67653589793e-4
SIN = (
    1.0,
    -0.16666655242443085,
    0.008333146572113037,
    -0.00019830558449029922,
    2.7278699690214125e-06,
    -2.1673399075439193e-08,
)
COS = (
    1.0,
    -0.4999999701976776,
    0.04166661947965622,
    -0.0013888514367863536,
    2.478722672094591e-05,
    -2.7273267733107787e-07,
    1.805915972319383e-09,
)

STEPS = 4
NF = 4
ROWS = 8
SLABS = 4
LAG = 1


def horner(coefs, x):
    total = coefs[-1] * x + coefs[-2]
    for coef in coefs[-3::-1]:
        total = total * x + coef
    return total


def cos_sin(phase):
    t = (phase - PI_HI) - PI_LO
    t2 = t * t
    return -horner(COS, t2), -(t * horner(SIN, t2))


def kernel(
    bands,
    src_hbm,
    rec_hbm,
    adj_hbm,
    slow_hbm,
    eps_hbm,
    del_hbm,
    slab_hbm,
    fidx_hbm,
    adj_out,
    img_out,
    grad_out,
    sed,
    model,
    msend,
    angb,
    first,
    sr,
    vsr,
    va,
    adj,
    cs,
    row_sr,
    halo_sr,
    row_a,
    halo_a,
    ipart,
    irecv,
    img,
    grad,
    gsend,
    grecv,
    gfin,
    gown,
    gsib,
    slab_ref,
    fidx_ref,
    stage,
    edge_send,
    edge_recv,
    edge_a_send,
    edge_a_recv,
    edge_raw,
    edge_near,
    slow_send,
    slow_recv,
    local_sem,
    send_sem,
    recv_sem,
    sr_send_sem,
    sr_recv_sem,
    edge_send_sem,
    edge_recv_sem,
    edge_a_send_sem,
    edge_a_recv_sem,
    slow_send_sem,
    slow_recv_sem,
):
    ni = sed.shape[-1]
    f = lax.axis_index("freq")
    b = lax.axis_index("xband")
    c = lax.rem(f, 2)
    o = 1 - c
    sib_f = f + 1 - 2 * c
    sib = (sib_f, b)
    far = (lax.rem(f + 2, 4), b)
    farx = (lax.rem(sib_f + 2, 4), b)
    neighbour = (sib_f, lax.rem(b + 2 * c - 1 + bands, bands))

    counts = {"local": 0, "remote": 0}

    def local_copy(source, target):
        k = counts["local"]
        counts["local"] += 1
        copy = pltpu.make_async_copy(source, target, local_sem.at[k])
        copy.start()
        return copy

    def remote_copy(source, target, device):
        k = counts["remote"]
        counts["remote"] += 1
        copy = pltpu.make_async_remote_copy(
            src_ref=source,
            dst_ref=target,
            send_sem=send_sem.at[k],
            recv_sem=recv_sem.at[k],
            device_id=device,
            device_id_type=MESH,
        )
        copy.start()
        return copy

    mine = pl.ds(pl.multiple_of(c * ROWS, ROWS), ROWS)
    theirs = pl.ds(pl.multiple_of(o * ROWS, ROWS), ROWS)
    my_slots = pl.ds(2 * c, 2)
    their_slots = pl.ds(2 * o, 2)

    outer_band = lax.rem(b + 2 * c - 1 + bands, bands)
    after_band = lax.rem(b + 1, bands)
    before_band = lax.rem(b + bands - 1, bands)
    chip = f // 2
    barrier = pltpu.get_barrier_semaphore()
    for device in [sib, far, farx] + [(k, outer_band) for k in range(4)]:
        pl.semaphore_signal(barrier, inc=1, device_id=device, device_id_type=MESH)

    ints = [local_copy(fidx_hbm, fidx_ref), local_copy(slab_hbm, slab_ref)]
    loads = [
        local_copy(ref.at[0], sed.at[k]) for k, ref in enumerate((slow_hbm, eps_hbm, del_hbm))
    ]
    fields_hbm = (src_hbm, rec_hbm, adj_hbm)
    stages = [local_copy(ref, stage.at[k]) for k, ref in enumerate(fields_hbm)]
    own_fields = [
        local_copy(ref.at[:, :, mine], first.at[k, my_slots]) for k, ref in enumerate(fields_hbm)
    ]

    ints[0].wait()
    for k in range(2):
        value = BASE_FREQ + FREQ_STEP * fidx_ref[k].astype(jnp.float32)
        angb[2 * c + k] = jnp.full((8, 128), value, jnp.float32)

    for copy in loads:
        copy.wait()
    for rows, ref in ((mine, model.at[f]), (theirs, msend)):
        slow = sed[0, rows]
        ref[0] = slow * (1.0 + sed[1, rows])
        ref[1] = (1.0 + 2.0 * sed[2, rows]) / slow
    for side, near, second in ((0, 0, 1), (1, 2 * ROWS - 1, 2 * ROWS - 2)):
        for n, row in enumerate((near, second)):
            slow_send[side, n] = sed[0, row : row + 1] * (1.0 + sed[1, row : row + 1])
        slow_send[side, 2] = (1.0 + 2.0 * sed[2, near : near + 1]) / sed[0, near : near + 1]
    def edge_copy(side, n, sender, device):
        return pltpu.make_async_remote_copy(
            src_ref=edge_send.at[side, n],
            dst_ref=edge_recv.at[sender, n],
            send_sem=edge_send_sem.at[side, n],
            recv_sem=edge_recv_sem.at[sender, n],
            device_id=device,
            device_id_type=MESH,
        )

    def edge_a_copy(side, sender, device):
        return pltpu.make_async_remote_copy(
            src_ref=edge_a_send.at[side],
            dst_ref=edge_a_recv.at[sender],
            send_sem=edge_a_send_sem.at[side],
            recv_sem=edge_a_recv_sem.at[sender],
            device_id=device,
            device_id_type=MESH,
        )

    def slow_copy(n, sender, device):
        return pltpu.make_async_remote_copy(
            src_ref=slow_send.at[n // 2],
            dst_ref=slow_recv.at[sender],
            send_sem=slow_send_sem.at[n],
            recv_sem=slow_recv_sem.at[sender],
            device_id=device,
            device_id_type=MESH,
        )

    pl.semaphore_wait(barrier, 7)
    sends = []
    models = [
        remote_copy(model.at[f], model.at[f], far),
        remote_copy(msend, model.at[f], farx),
        remote_copy(msend, model.at[f], sib),
    ]
    before, after = (2 * chip + 1, before_band), (2 * chip, after_band)
    slows = [
        slow_copy(0, f, (1, before_band)),
        slow_copy(1, f, (3, before_band)),
        slow_copy(2, f, (0, after_band)),
        slow_copy(3, f, (2, after_band)),
    ]
    nears = [edge_copy(0, 0, c, before), edge_copy(1, 0, c, after)]
    seconds = [
        edge_a_copy(0, c, before),
        edge_a_copy(1, c, after),
        edge_copy(0, 1, c, before),
        edge_copy(1, 1, c, after),
    ]
    for copy in slows:
        copy.start()
    for copy in stages:
        copy.wait()

    def pack(n, row_of):
        for side in range(2):
            row = row_of[side]
            for field in range(2):
                for k in range(2):
                    for part in range(2):
                        at = 2 * field + k
                        edge_send[side, n, part, at : at + 1] = stage[field, k, part, row : row + 1]

    pack(0, (0, 2 * ROWS - 1))
    for copy in nears:
        copy.start()
    angs = remote_copy(angb.at[my_slots], angb.at[my_slots], sib)
    fields = [
        remote_copy(ref.at[:, :, theirs], first.at[k, my_slots], sib)
        for k, ref in enumerate(fields_hbm)
    ]
    sends += models[2:] + [angs] + fields + slows + seconds
    pack(1, (1, 2 * ROWS - 2))
    for side, row in ((0, 0), (1, 2 * ROWS - 1)):
        for k in range(2):
            for part in range(2):
                edge_a_send[side, part, k : k + 1] = stage[2, k, part, row : row + 1]
    for copy in models[:2] + nears:
        copy.wait_send()
    for copy in seconds:
        copy.start()
    for copy in [angs] + models:
        copy.wait_recv()

    ints[1].wait()
    slabs = [slab_ref[z] for z in range(STEPS)]
    lanes = lax.broadcasted_iota(jnp.int32, (ROWS, 128), 1)
    sublanes = lax.broadcasted_iota(jnp.int32, (ROWS, ni), 0)
    top_row = sublanes == 0
    last_row = sublanes == ROWS - 1
    keep_top = jnp.where((c == 0) & (b == 0), 0.0, 1.0)
    keep_last = jnp.where((c == 1) & (b == bands - 1), 0.0, 1.0)

    def wide(tile):
        return jnp.concatenate([tile] * (ni // 128), axis=1)

    def trig(z):
        def body(k, carry):
            cosine, sine = cos_sin(wide(angb[k]) * model[slabs[z], 0])
            cs[z, k, 0] = cosine
            cs[z, k, 1] = sine
            return carry

        lax.fori_loop(0, NF, body, 0)

    def rotate(p, q, cosine, sine, sign):
        if sign > 0:
            return p * cosine - q * sine, p * sine + q * cosine
        return p * cosine + q * sine, q * cosine - p * sine

    def put_rows(rows, z, k, j, value):
        rows[z, 0, k, pl.ds(j, 1), :] = value[0:1, :]
        rows[z, 1, k, pl.ds(j, 1), :] = value[ROWS - 1 : ROWS, :]

    def around(v, halos, z, k, j):
        top = halos[z, 0, k, pl.ds(j, 1), :] * keep_top
        last = halos[z, 1, k, pl.ds(j, 1), :] * keep_last
        above = jnp.where(top_row, top, pltpu.roll(v, 1, 0))
        below = jnp.where(last_row, last, pltpu.roll(v, ROWS - 1, 0))
        before = pltpu.roll(v, 1, 1)
        before = jnp.concatenate(
            [jnp.where(lanes == 0, 0.0, before[:, :128]), before[:, 128:]], axis=1
        )
        after = pltpu.roll(v, ni - 1, 1)
        after = jnp.concatenate(
            [after[:, :-128], jnp.where(lanes == 127, 0.0, after[:, -128:])], axis=1
        )
        return (above + below) + (before + after)

    def spread(vr, vi, halos, z, k, j, coupling):
        lap_r = around(vr, halos, z, k, j) - 4.0 * vr
        lap_i = around(vi, halos, z, k, j + 1) - 4.0 * vi
        return (
            vr + DIFFUSE * lap_r - coupling * lap_i,
            vi + DIFFUSE * lap_i + coupling * lap_r,
        )

    def couple(z, k):
        return wide(DISPERSE * BASE_FREQ / angb[k]) * model[slabs[z], 1]

    def rotate_sr(z, k, values):
        cosine, sine = cs[z, k, 0], cs[z, k, 1]
        rotated = rotate(values[0], values[1], cosine, sine, 1) + rotate(
            values[2], values[3], cosine, sine, -1
        )
        for j, value in enumerate(rotated):
            vsr[k, j] = value
            put_rows(row_sr, z, k, j, value)

    def rotate_a(z, k, real, imag):
        rotated = rotate(real, imag, cs[z, k, 0], cs[z, k, 1], -1)
        for j, value in enumerate(rotated):
            va[k, j] = value
            put_rows(row_a, z, k, j, value)

    def send_rows(rows, halos, z):
        return [
            remote_copy(rows.at[z, c], halos.at[z, o], neighbour),
            remote_copy(rows.at[z, o], halos.at[z, c], sib),
        ]

    def sr_outer(z, k):
        return pltpu.make_async_remote_copy(
            src_ref=row_sr.at[z, c, k],
            dst_ref=halo_sr.at[z, o, k],
            send_sem=sr_send_sem.at[z, k, 0],
            recv_sem=sr_recv_sem.at[z, k, 0],
            device_id=neighbour,
            device_id_type=MESH,
        )

    def sr_inner(z, k):
        return pltpu.make_async_remote_copy(
            src_ref=row_sr.at[z, o, k],
            dst_ref=halo_sr.at[z, c, k],
            send_sem=sr_send_sem.at[z, k, 1],
            recv_sem=sr_recv_sem.at[z, k, 1],
            device_id=sib,
            device_id_type=MESH,
        )

    rows8 = lax.broadcasted_iota(jnp.int32, (8, 128), 0)
    edge_ang = jnp.where(
        rows8 < 4,
        jnp.where(rows8 % 2 == 0, angb[0], angb[1]),
        jnp.where(rows8 % 2 == 0, angb[2], angb[3]),
    )
    edge_sign = wide(jnp.where(rows8 % 4 < 2, 1.0, -1.0))

    def edge_rotated(n, cosine, sine):
        for core in range(2):
            for part in range(2):
                edge_raw[n, part, 4 * core : 4 * core + 4] = edge_recv[core, n, part]
        p, q = edge_raw[n, 0], edge_raw[n, 1]
        return p * cosine - q * sine, p * sine + q * cosine

    def put_edges(z, real, imag):
        for core in range(2):
            for field in range(2):
                for k in range(2):
                    at = 4 * core + 2 * field + k
                    for part, value in enumerate((real, imag)):
                        j = 2 * field + part
                        halo_sr[z, c, 2 * core + k, j : j + 1] = value[at : at + 1]

    def first_edges():
        cosine, sine = cos_sin(wide(edge_ang) * slow_recv[slabs[0], 0])
        real, imag = edge_rotated(0, cosine, sine * edge_sign)
        edge_near[0] = real
        edge_near[1] = imag
        put_edges(0, real, imag)

    def beside(v):
        before = pltpu.roll(v, 1, 1)
        before = jnp.concatenate(
            [jnp.where(lanes == 0, 0.0, before[:, :128]), before[:, 128:]], axis=1
        )
        after = pltpu.roll(v, ni - 1, 1)
        after = jnp.concatenate(
            [after[:, :-128], jnp.where(lanes == 127, 0.0, after[:, -128:])], axis=1
        )
        return before + after

    def second_edges():
        cosine, sine = cos_sin(wide(edge_ang) * slow_recv[slabs[0], 1])
        far_r, far_i = edge_rotated(1, cosine, sine * edge_sign)
        for core in range(2):
            for field in range(2):
                for k in range(2):
                    at = 4 * core + 2 * field + k
                    for part in range(2):
                        j = 2 * field + part
                        edge_raw[0, part, at : at + 1] = row_sr[0, c, 2 * core + k, j : j + 1]
        vr, vi = edge_near[0], edge_near[1]
        lap_r = (edge_raw[0, 0] + far_r) + beside(vr) - 4.0 * vr
        lap_i = (edge_raw[0, 1] + far_i) + beside(vi) - 4.0 * vi
        coupling = edge_sign * wide(DISPERSE * BASE_FREQ / edge_ang) * slow_recv[slabs[0], 2]
        p = vr + DIFFUSE * lap_r - coupling * lap_i
        q = vi + DIFFUSE * lap_i + coupling * lap_r
        cosine, sine = cos_sin(wide(edge_ang) * slow_recv[slabs[1], 0])
        sine = sine * edge_sign
        put_edges(1, p * cosine - q * sine, p * sine + q * cosine)

    def adjoint_edges():
        cosine, sine = cos_sin(wide(edge_ang) * slow_recv[slabs[0], 0])
        for core in range(2):
            for part in range(2):
                for twice in range(2):
                    at = 4 * core + 2 * twice
                    edge_raw[2, part, at : at + 2] = edge_a_recv[core, part]
        p, q = edge_raw[2, 0], edge_raw[2, 1]
        for part, value in enumerate((p * cosine + q * sine, q * cosine - p * sine)):
            for core in range(2):
                for k in range(2):
                    at = 4 * core + k
                    halo_a[0, c, 2 * core + k, part : part + 1] = value[at : at + 1]

    def first_sr(k, carry):
        rotate_sr(0, k, (first[0, k, 0], first[0, k, 1], first[1, k, 0], first[1, k, 1]))
        sr_inner(0, k).start()
        return carry

    def first_a(k, carry):
        rotate_a(0, k, first[2, k, 0], first[2, k, 1])
        return carry

    def pass_sr(z):
        def body(k, total):
            coupling = couple(z, k)
            if z > 1:
                sr_outer(z, k).wait_recv()
            sr_inner(z, k).wait_recv()
            s_r, s_i = spread(vsr[k, 0], vsr[k, 1], halo_sr, z, k, 0, coupling)
            r_r, r_i = spread(vsr[k, 2], vsr[k, 3], halo_sr, z, k, 2, -coupling)
            for j, value in enumerate((s_r, s_i, r_r, r_i)):
                sr[z, k, j] = value
            if z + 1 < STEPS:
                rotate_sr(z + 1, k, (s_r, s_i, r_r, r_i))
                if z > 0:
                    sr_outer(z + 1, k).start()
                sr_inner(z + 1, k).start()
            return total + (s_r * r_r + s_i * r_i)

        ipart[z] = lax.fori_loop(0, NF, body, jnp.zeros((ROWS, ni), jnp.float32))

    def pass_a(z):
        def body(k, carry):
            a_r, a_i = spread(va[k, 0], va[k, 1], halo_a, z, k, 0, -couple(z, k))
            adj[k, 0] = a_r
            adj[k, 1] = a_i
            return carry

        lax.fori_loop(0, NF, body, 0)

    def force(z):
        def body(k, totals):
            ang = wide(angb[k])
            inv = wide(BASE_FREQ / angb[k])
            s_r, s_i, r_r, r_i = (sr[z, k, j] for j in range(4))
            half = FORCING * img[z]
            a_r = adj[k, 0] + half * s_r
            a_i = adj[k, 1] + half * s_i
            if z + 1 < STEPS:
                rotate_a(z + 1, k, a_r, a_i)
            else:
                adj[k, 0] = a_r
                adj[k, 1] = a_i
            grad[z, 0] = jnp.where(k == 0, 0.0, grad[z, 0]) + ang * (s_r * a_i - s_i * a_r)
            grad[z, 1] = jnp.where(k == 0, 0.0, grad[z, 1]) + ang * (r_r * a_i - r_i * a_r)
            grad[z, 2] = jnp.where(k == 0, 0.0, grad[z, 2]) + inv * (s_r * a_r + s_i * a_i)
            return totals

        lax.fori_loop(0, NF, body, 0)

    trig(0)
    for copy in own_fields[:2]:
        copy.wait()
    for copy in fields[:2]:
        copy.wait_recv()
    lax.fori_loop(0, NF, first_sr, 0)
    for core in range(2):
        edge_copy(0, 0, core, sib).wait_recv()
    for k in range(SLABS):
        slow_copy(0, k, sib).wait_recv()
    first_edges()
    trig(1)

    def uses(chip):
        at = []
        for j in range(2):
            step = 0
            for z in range(1, STEPS):
                step = jnp.where(slabs[z] == 2 * chip + j, z, step)
            at.append(step)
        return jnp.minimum(at[0], at[1]), jnp.maximum(at[0], at[1]), at[0] < at[1]

    far_uses = uses(1 - chip)
    my_uses = uses(chip)
    copies = []
    arrivals = []
    gradients = []

    def finish(z, wait_a, image):
        for copy in wait_a:
            copy.wait_recv()
        pass_a(z)
        image.wait_recv()
        img[z] = (ipart[z] + irecv[z]) * (1.0 / (2 * NF))
        force(z)
        wait_a = []
        if z + 1 < STEPS:
            wait_a = send_rows(row_a, halo_a, z + 1)
            sends.extend(wait_a)
        if z >= STEPS - 2:
            n = z - (STEPS - 2)
            for j in range(3):
                gsend[n, j] = grad[far_uses[n], j]
                gradients.append(remote_copy(gsend.at[n, j], grecv.at[n, j], far))
        if z + 1 == STEPS:
            arrivals.append(remote_copy(adj.at[their_slots], adj_out.at[:, :, mine], sib))
            copies.append(local_copy(adj.at[my_slots], adj_out.at[:, :, mine]))
        copies.append(local_copy(img.at[z], img_out.at[z, mine]))
        arrivals.append(remote_copy(img.at[z], img_out.at[z, mine], sib))
        return wait_a

    images = []
    for z in range(STEPS):
        pass_sr(z)
        images.append(remote_copy(ipart.at[z], irecv.at[z], far))
        if z == 0:
            own_fields[2].wait()
            fields[2].wait_recv()
            lax.fori_loop(0, NF, first_a, 0)
            wait_a = [remote_copy(row_a.at[0, o], halo_a.at[0, c], sib)]
            sends += wait_a
        if z == 0:
            for core in range(2):
                edge_a_copy(0, core, sib).wait_recv()
                edge_copy(0, 1, core, sib).wait_recv()
            second_edges()
        if z == 1:
            adjoint_edges()
        if z + 2 < STEPS:
            trig(z + 2)
        if LAG == 0:
            wait_a = finish(z, wait_a, images[z])
        elif z > 0:
            wait_a = finish(z - 1, wait_a, images[z - 1])
    if LAG:
        wait_a = finish(STEPS - 1, wait_a, images[STEPS - 1])
    sends += images
    sends += gradients

    first_is_zero = my_uses[2].astype(jnp.int32)
    own_is = jnp.where(c == 0, 1 - first_is_zero, first_is_zero)
    for j in range(3):
        for n in range(2):
            gradients[3 * n + j].wait_recv()
            gfin[n, j] = (grad[my_uses[n], j] + grecv[n, j]) * (1.0 / (2 * NF))
        gsib[j] = gfin[1 - own_is, j]
        arrivals.append(remote_copy(gsib.at[j], grad_out.at[0, j, mine], sib))
        gown[j] = gfin[own_is, j]
        copies.append(local_copy(gown.at[j], grad_out.at[0, j, mine]))
    for copy in arrivals:
        copy.wait_recv()
    for copy in copies:
        copy.wait()
    for copy in sends + arrivals:
        copy.wait_send()
    for z in range(STEPS):
        for k in range(NF):
            if z > 1:
                sr_outer(z, k).wait_send()
            sr_inner(z, k).wait_send()


def hand_over(*refs):
    copies = [
        pltpu.make_async_copy(refs[k], refs[3 + k], refs[6].at[k]) for k in range(3)
    ]
    for copy in copies:
        copy.start()
    for copy in copies:
        copy.wait()


def solution(mesh):
    bands = mesh.shape["xband"]

    def step(*args):
        args = [pltpu.with_memory_space_constraint(x, pltpu.HBM) for x in args]
        ni = args[0].shape[-1]
        half = (ROWS, ni)
        f32 = jnp.float32

        def vmem(*shape):
            return pltpu.VMEM(shape, f32)

        scratch = [
            vmem(3, 2 * ROWS, ni),
            vmem(SLABS, 2, *half),
            vmem(2, *half),
            vmem(NF, 8, 128),
            vmem(3, NF, 2, *half),
            vmem(STEPS, NF, 4, *half),
            vmem(NF, 4, *half),
            vmem(NF, 2, *half),
            vmem(NF, 2, *half),
            vmem(STEPS, NF, 2, *half),
            vmem(STEPS, 2, NF, 4, ni),
            vmem(STEPS, 2, NF, 4, ni),
            vmem(STEPS, 2, NF, 2, ni),
            vmem(STEPS, 2, NF, 2, ni),
            vmem(STEPS, *half),
            vmem(STEPS, *half),
            vmem(STEPS, *half),
            vmem(STEPS, 3, *half),
            vmem(2, 3, *half),
            vmem(2, 3, *half),
            vmem(2, 3, *half),
            vmem(3, *half),
            vmem(3, *half),
            pltpu.SMEM(args[6].shape, jnp.int32),
            pltpu.SMEM(args[7].shape, jnp.int32),
            vmem(3, 2, 2, 2 * ROWS, ni),
            vmem(2, 2, 2, 4, ni),
            vmem(2, 2, 2, 4, ni),
            vmem(2, 2, 2, ni),
            vmem(2, 2, 2, ni),
            vmem(3, 2, 8, ni),
            vmem(2, 8, ni),
            vmem(2, 3, 1, ni),
            vmem(SLABS, 3, 1, ni),
            pltpu.SemaphoreType.DMA((24,)),
            pltpu.SemaphoreType.DMA((40,)),
            pltpu.SemaphoreType.DMA((40,)),
            pltpu.SemaphoreType.DMA((STEPS, NF, 2)),
            pltpu.SemaphoreType.DMA((STEPS, NF, 2)),
            pltpu.SemaphoreType.DMA((2, 2)),
            pltpu.SemaphoreType.DMA((2, 2)),
            pltpu.SemaphoreType.DMA((2,)),
            pltpu.SemaphoreType.DMA((2,)),
            pltpu.SemaphoreType.DMA((4,)),
            pltpu.SemaphoreType.DMA((SLABS,)),
        ]
        any_spec = pl.BlockSpec(memory_space=pl.ANY)
        hbm_spec = pl.BlockSpec(memory_space=pltpu.HBM)
        outs = pl.pallas_call(
            functools.partial(kernel, bands),
            out_shape=(
                jax.ShapeDtypeStruct(args[2].shape, f32),
                jax.ShapeDtypeStruct((STEPS,) + args[3].shape[1:], f32),
                jax.ShapeDtypeStruct((1, 3) + args[3].shape[1:], f32),
            ),
            in_specs=[hbm_spec] * 8,
            out_specs=(any_spec,) * 3,
            scratch_shapes=scratch,
            compiler_params=pltpu.CompilerParams(
                collective_id=0, has_side_effects=True, vmem_limit_bytes=40 * 2**20
            ),
        )(*args)
        return pl.pallas_call(
            hand_over,
            out_shape=tuple(jax.ShapeDtypeStruct(x.shape, f32) for x in outs),
            in_specs=[any_spec] * 3,
            out_specs=(any_spec,) * 3,
            scratch_shapes=[pltpu.SemaphoreType.DMA((3,))],
            compiler_params=pltpu.CompilerParams(vmem_limit_bytes=4 * 2**20),
        )(*outs)

    return jax.shard_map(
        step,
        mesh=mesh,
        in_specs=(
            P("freq", None, "xband", None),
            P("freq", None, "xband", None),
            P("freq", None, "xband", None),
            P("freq", "xband", None),
            P("freq", "xband", None),
            P("freq", "xband", None),
            P(),
            P("freq"),
        ),
        out_specs=(
            P("freq", None, "xband", None),
            P(None, "xband", None),
            P("freq", None, "xband", None),
        ),
        check_vma=False,
    )
```

```python
import functools

import jax
import jax.numpy as jnp
from jax import lax
from jax.experimental import pallas as pl
from jax.experimental.pallas import tpu as pltpu
from jax.sharding import PartitionSpec as P

BASE_FREQ = 2.0
FREQ_STEP = 0.25
DISPERSE = 0.08
DIFFUSE = 0.05
FORCING = 0.5
MESH = pl.DeviceIdType.MESH

PI_HI = 3.140625
PI_LO = 9.67653589793e-4
SIN = (
    1.0,
    -0.16666655242443085,
    0.008333146572113037,
    -0.00019830558449029922,
    2.7278699690214125e-06,
    -2.1673399075439193e-08,
)
COS = (
    1.0,
    -0.4999999701976776,
    0.04166661947965622,
    -0.0013888514367863536,
    2.478722672094591e-05,
    -2.7273267733107787e-07,
    1.805915972319383e-09,
)

STEPS = 4
NF = 4
ROWS = 8
SLABS = 4
LAG = 1


def horner(coefs, x):
    total = coefs[-1] * x + coefs[-2]
    for coef in coefs[-3::-1]:
        total = total * x + coef
    return total


def cos_sin(phase):
    t = (phase - PI_HI) - PI_LO
    t2 = t * t
    return -horner(COS, t2), -(t * horner(SIN, t2))


def kernel(
    bands,
    src_hbm,
    rec_hbm,
    adj_hbm,
    slow_hbm,
    eps_hbm,
    del_hbm,
    slab_hbm,
    fidx_hbm,
    adj_out,
    img_out,
    grad_out,
    sed,
    model,
    msend,
    angb,
    first,
    sr,
    vsr,
    va,
    adj,
    cs,
    row_sr,
    halo_sr,
    row_a,
    halo_a,
    ipart,
    irecv,
    img,
    grad,
    gsend,
    grecv,
    gfin,
    gown,
    gsib,
    slab_ref,
    fidx_ref,
    stage,
    edge_send,
    edge_recv,
    edge_a_send,
    edge_a_recv,
    edge_raw,
    edge_near,
    slow_send,
    slow_recv,
    local_sem,
    send_sem,
    recv_sem,
    sr_send_sem,
    sr_recv_sem,
    a_send_sem,
    a_recv_sem,
    edge_send_sem,
    edge_recv_sem,
    edge_a_send_sem,
    edge_a_recv_sem,
    slow_send_sem,
    slow_recv_sem,
):
    ni = sed.shape[-1]
    f = lax.axis_index("freq")
    b = lax.axis_index("xband")
    c = lax.rem(f, 2)
    o = 1 - c
    sib_f = f + 1 - 2 * c
    sib = (sib_f, b)
    far = (lax.rem(f + 2, 4), b)
    farx = (lax.rem(sib_f + 2, 4), b)
    neighbour = (sib_f, lax.rem(b + 2 * c - 1 + bands, bands))

    counts = {"local": 0, "remote": 0}

    def local_copy(source, target):
        k = counts["local"]
        counts["local"] += 1
        copy = pltpu.make_async_copy(source, target, local_sem.at[k])
        copy.start()
        return copy

    def remote_copy(source, target, device):
        k = counts["remote"]
        counts["remote"] += 1
        copy = pltpu.make_async_remote_copy(
            src_ref=source,
            dst_ref=target,
            send_sem=send_sem.at[k],
            recv_sem=recv_sem.at[k],
            device_id=device,
            device_id_type=MESH,
        )
        copy.start()
        return copy

    mine = pl.ds(pl.multiple_of(c * ROWS, ROWS), ROWS)
    theirs = pl.ds(pl.multiple_of(o * ROWS, ROWS), ROWS)
    my_slots = pl.ds(2 * c, 2)
    their_slots = pl.ds(2 * o, 2)

    outer_band = lax.rem(b + 2 * c - 1 + bands, bands)
    after_band = lax.rem(b + 1, bands)
    before_band = lax.rem(b + bands - 1, bands)
    chip = f // 2
    barrier = pltpu.get_barrier_semaphore()
    for device in [sib, far, farx] + [(k, outer_band) for k in range(4)]:
        pl.semaphore_signal(barrier, inc=1, device_id=device, device_id_type=MESH)

    ints = [local_copy(fidx_hbm, fidx_ref), local_copy(slab_hbm, slab_ref)]
    loads = [
        local_copy(ref.at[0], sed.at[k]) for k, ref in enumerate((slow_hbm, eps_hbm, del_hbm))
    ]
    fields_hbm = (src_hbm, rec_hbm, adj_hbm)
    stages = [local_copy(ref, stage.at[k]) for k, ref in enumerate(fields_hbm)]
    own_fields = [
        local_copy(ref.at[:, :, mine], first.at[k, my_slots]) for k, ref in enumerate(fields_hbm)
    ]

    ints[0].wait()
    for k in range(2):
        value = BASE_FREQ + FREQ_STEP * fidx_ref[k].astype(jnp.float32)
        angb[2 * c + k] = jnp.full((8, 128), value, jnp.float32)

    for copy in loads:
        copy.wait()
    for rows, ref in ((mine, model.at[f]), (theirs, msend)):
        slow = sed[0, rows]
        ref[0] = slow * (1.0 + sed[1, rows])
        ref[1] = (1.0 + 2.0 * sed[2, rows]) / slow
    for side, near, second in ((0, 0, 1), (1, 2 * ROWS - 1, 2 * ROWS - 2)):
        for n, row in enumerate((near, second)):
            slow_send[side, n] = sed[0, row : row + 1] * (1.0 + sed[1, row : row + 1])
        slow_send[side, 2] = (1.0 + 2.0 * sed[2, near : near + 1]) / sed[0, near : near + 1]
    def edge_copy(side, n, sender, device):
        return pltpu.make_async_remote_copy(
            src_ref=edge_send.at[side, n],
            dst_ref=edge_recv.at[sender, n],
            send_sem=edge_send_sem.at[side, n],
            recv_sem=edge_recv_sem.at[sender, n],
            device_id=device,
            device_id_type=MESH,
        )

    def edge_a_copy(side, sender, device):
        return pltpu.make_async_remote_copy(
            src_ref=edge_a_send.at[side],
            dst_ref=edge_a_recv.at[sender],
            send_sem=edge_a_send_sem.at[side],
            recv_sem=edge_a_recv_sem.at[sender],
            device_id=device,
            device_id_type=MESH,
        )

    def slow_copy(n, sender, device):
        return pltpu.make_async_remote_copy(
            src_ref=slow_send.at[n // 2],
            dst_ref=slow_recv.at[sender],
            send_sem=slow_send_sem.at[n],
            recv_sem=slow_recv_sem.at[sender],
            device_id=device,
            device_id_type=MESH,
        )

    pl.semaphore_wait(barrier, 7)
    sends = []
    models = [
        remote_copy(model.at[f], model.at[f], far),
        remote_copy(msend, model.at[f], farx),
        remote_copy(msend, model.at[f], sib),
    ]
    before, after = (2 * chip + 1, before_band), (2 * chip, after_band)
    slows = [
        slow_copy(0, f, (1, before_band)),
        slow_copy(1, f, (3, before_band)),
        slow_copy(2, f, (0, after_band)),
        slow_copy(3, f, (2, after_band)),
    ]
    nears = [edge_copy(0, 0, c, before), edge_copy(1, 0, c, after)]
    seconds = [
        edge_a_copy(0, c, before),
        edge_a_copy(1, c, after),
        edge_copy(0, 1, c, before),
        edge_copy(1, 1, c, after),
    ]
    for copy in slows:
        copy.start()
    for copy in stages:
        copy.wait()

    def pack(n, row_of):
        for side in range(2):
            row = row_of[side]
            for field in range(2):
                for k in range(2):
                    for part in range(2):
                        at = 2 * field + k
                        edge_send[side, n, part, at : at + 1] = stage[field, k, part, row : row + 1]

    pack(0, (0, 2 * ROWS - 1))
    for copy in nears:
        copy.start()
    angs = remote_copy(angb.at[my_slots], angb.at[my_slots], sib)
    fields = [
        remote_copy(ref.at[:, :, theirs], first.at[k, my_slots], sib)
        for k, ref in enumerate(fields_hbm)
    ]
    sends += models[2:] + [angs] + fields + slows + seconds
    pack(1, (1, 2 * ROWS - 2))
    for side, row in ((0, 0), (1, 2 * ROWS - 1)):
        for k in range(2):
            for part in range(2):
                edge_a_send[side, part, k : k + 1] = stage[2, k, part, row : row + 1]
    for copy in models[:2] + nears:
        copy.wait_send()
    for copy in seconds:
        copy.start()
    for copy in [angs] + models:
        copy.wait_recv()

    ints[1].wait()
    slabs = [slab_ref[z] for z in range(STEPS)]
    lanes = lax.broadcasted_iota(jnp.int32, (ROWS, 128), 1)
    sublanes = lax.broadcasted_iota(jnp.int32, (ROWS, ni), 0)
    top_row = sublanes == 0
    last_row = sublanes == ROWS - 1
    keep_top = jnp.where((c == 0) & (b == 0), 0.0, 1.0)
    keep_last = jnp.where((c == 1) & (b == bands - 1), 0.0, 1.0)

    def wide(tile):
        return jnp.concatenate([tile] * (ni // 128), axis=1)

    def trig(z):
        def body(k, carry):
            cosine, sine = cos_sin(wide(angb[k]) * model[slabs[z], 0])
            cs[z, k, 0] = cosine
            cs[z, k, 1] = sine
            return carry

        lax.fori_loop(0, NF, body, 0)

    def rotate(p, q, cosine, sine, sign):
        if sign > 0:
            return p * cosine - q * sine, p * sine + q * cosine
        return p * cosine + q * sine, q * cosine - p * sine

    def put_rows(rows, z, k, j, value):
        rows[z, 0, k, pl.ds(j, 1), :] = value[0:1, :]
        rows[z, 1, k, pl.ds(j, 1), :] = value[ROWS - 1 : ROWS, :]

    def around(v, halos, z, k, j):
        top = halos[z, 0, k, pl.ds(j, 1), :] * keep_top
        last = halos[z, 1, k, pl.ds(j, 1), :] * keep_last
        above = jnp.where(top_row, top, pltpu.roll(v, 1, 0))
        below = jnp.where(last_row, last, pltpu.roll(v, ROWS - 1, 0))
        before = pltpu.roll(v, 1, 1)
        before = jnp.concatenate(
            [jnp.where(lanes == 0, 0.0, before[:, :128]), before[:, 128:]], axis=1
        )
        after = pltpu.roll(v, ni - 1, 1)
        after = jnp.concatenate(
            [after[:, :-128], jnp.where(lanes == 127, 0.0, after[:, -128:])], axis=1
        )
        return (above + below) + (before + after)

    def spread(vr, vi, halos, z, k, j, coupling):
        lap_r = around(vr, halos, z, k, j) - 4.0 * vr
        lap_i = around(vi, halos, z, k, j + 1) - 4.0 * vi
        return (
            vr + DIFFUSE * lap_r - coupling * lap_i,
            vi + DIFFUSE * lap_i + coupling * lap_r,
        )

    def couple(z, k):
        return wide(DISPERSE * BASE_FREQ / angb[k]) * model[slabs[z], 1]

    def rotate_sr(z, k, values):
        cosine, sine = cs[z, k, 0], cs[z, k, 1]
        rotated = rotate(values[0], values[1], cosine, sine, 1) + rotate(
            values[2], values[3], cosine, sine, -1
        )
        for j, value in enumerate(rotated):
            vsr[k, j] = value
            put_rows(row_sr, z, k, j, value)

    def rotate_a(z, k, real, imag):
        rotated = rotate(real, imag, cs[z, k, 0], cs[z, k, 1], -1)
        for j, value in enumerate(rotated):
            va[k, j] = value
            put_rows(row_a, z, k, j, value)

    def a_outer(z, k):
        return pltpu.make_async_remote_copy(
            src_ref=row_a.at[z, c, k],
            dst_ref=halo_a.at[z, o, k],
            send_sem=a_send_sem.at[z, k, 0],
            recv_sem=a_recv_sem.at[z, k, 0],
            device_id=neighbour,
            device_id_type=MESH,
        )

    def a_inner(z, k):
        return pltpu.make_async_remote_copy(
            src_ref=row_a.at[z, o, k],
            dst_ref=halo_a.at[z, c, k],
            send_sem=a_send_sem.at[z, k, 1],
            recv_sem=a_recv_sem.at[z, k, 1],
            device_id=sib,
            device_id_type=MESH,
        )

    def sr_outer(z, k):
        return pltpu.make_async_remote_copy(
            src_ref=row_sr.at[z, c, k],
            dst_ref=halo_sr.at[z, o, k],
            send_sem=sr_send_sem.at[z, k, 0],
            recv_sem=sr_recv_sem.at[z, k, 0],
            device_id=neighbour,
            device_id_type=MESH,
        )

    def sr_inner(z, k):
        return pltpu.make_async_remote_copy(
            src_ref=row_sr.at[z, o, k],
            dst_ref=halo_sr.at[z, c, k],
            send_sem=sr_send_sem.at[z, k, 1],
            recv_sem=sr_recv_sem.at[z, k, 1],
            device_id=sib,
            device_id_type=MESH,
        )

    rows8 = lax.broadcasted_iota(jnp.int32, (8, 128), 0)
    edge_ang = jnp.where(
        rows8 < 4,
        jnp.where(rows8 % 2 == 0, angb[0], angb[1]),
        jnp.where(rows8 % 2 == 0, angb[2], angb[3]),
    )
    edge_sign = wide(jnp.where(rows8 % 4 < 2, 1.0, -1.0))

    def edge_rotated(n, cosine, sine):
        for core in range(2):
            for part in range(2):
                edge_raw[n, part, 4 * core : 4 * core + 4] = edge_recv[core, n, part]
        p, q = edge_raw[n, 0], edge_raw[n, 1]
        return p * cosine - q * sine, p * sine + q * cosine

    def put_edges(z, real, imag):
        for core in range(2):
            for field in range(2):
                for k in range(2):
                    at = 4 * core + 2 * field + k
                    for part, value in enumerate((real, imag)):
                        j = 2 * field + part
                        halo_sr[z, c, 2 * core + k, j : j + 1] = value[at : at + 1]

    def first_edges():
        cosine, sine = cos_sin(wide(edge_ang) * slow_recv[slabs[0], 0])
        real, imag = edge_rotated(0, cosine, sine * edge_sign)
        edge_near[0] = real
        edge_near[1] = imag
        put_edges(0, real, imag)

    def beside(v):
        before = pltpu.roll(v, 1, 1)
        before = jnp.concatenate(
            [jnp.where(lanes == 0, 0.0, before[:, :128]), before[:, 128:]], axis=1
        )
        after = pltpu.roll(v, ni - 1, 1)
        after = jnp.concatenate(
            [after[:, :-128], jnp.where(lanes == 127, 0.0, after[:, -128:])], axis=1
        )
        return before + after

    def second_edges():
        cosine, sine = cos_sin(wide(edge_ang) * slow_recv[slabs[0], 1])
        far_r, far_i = edge_rotated(1, cosine, sine * edge_sign)
        for core in range(2):
            for field in range(2):
                for k in range(2):
                    at = 4 * core + 2 * field + k
                    for part in range(2):
                        j = 2 * field + part
                        edge_raw[0, part, at : at + 1] = row_sr[0, c, 2 * core + k, j : j + 1]
        vr, vi = edge_near[0], edge_near[1]
        lap_r = (edge_raw[0, 0] + far_r) + beside(vr) - 4.0 * vr
        lap_i = (edge_raw[0, 1] + far_i) + beside(vi) - 4.0 * vi
        coupling = edge_sign * wide(DISPERSE * BASE_FREQ / edge_ang) * slow_recv[slabs[0], 2]
        p = vr + DIFFUSE * lap_r - coupling * lap_i
        q = vi + DIFFUSE * lap_i + coupling * lap_r
        cosine, sine = cos_sin(wide(edge_ang) * slow_recv[slabs[1], 0])
        sine = sine * edge_sign
        put_edges(1, p * cosine - q * sine, p * sine + q * cosine)

    def adjoint_edges():
        cosine, sine = cos_sin(wide(edge_ang) * slow_recv[slabs[0], 0])
        for core in range(2):
            for part in range(2):
                for twice in range(2):
                    at = 4 * core + 2 * twice
                    edge_raw[2, part, at : at + 2] = edge_a_recv[core, part]
        p, q = edge_raw[2, 0], edge_raw[2, 1]
        for part, value in enumerate((p * cosine + q * sine, q * cosine - p * sine)):
            for core in range(2):
                for k in range(2):
                    at = 4 * core + k
                    halo_a[0, c, 2 * core + k, part : part + 1] = value[at : at + 1]

    def first_sr(k, carry):
        rotate_sr(0, k, (first[0, k, 0], first[0, k, 1], first[1, k, 0], first[1, k, 1]))
        sr_inner(0, k).start()
        return carry

    def first_a(k, carry):
        rotate_a(0, k, first[2, k, 0], first[2, k, 1])
        a_inner(0, k).start()
        return carry

    def pass_sr(z):
        def body(k, total):
            coupling = couple(z, k)
            if z > 1:
                sr_outer(z, k).wait_recv()
            sr_inner(z, k).wait_recv()
            s_r, s_i = spread(vsr[k, 0], vsr[k, 1], halo_sr, z, k, 0, coupling)
            r_r, r_i = spread(vsr[k, 2], vsr[k, 3], halo_sr, z, k, 2, -coupling)
            for j, value in enumerate((s_r, s_i, r_r, r_i)):
                sr[z, k, j] = value
            if z + 1 < STEPS:
                rotate_sr(z + 1, k, (s_r, s_i, r_r, r_i))
                if z > 0:
                    sr_outer(z + 1, k).start()
                sr_inner(z + 1, k).start()
            return total + (s_r * r_r + s_i * r_i)

        ipart[z] = lax.fori_loop(0, NF, body, jnp.zeros((ROWS, ni), jnp.float32))

    def pass_a(z):
        def body(k, carry):
            if z > 0:
                a_outer(z, k).wait_recv()
            a_inner(z, k).wait_recv()
            a_r, a_i = spread(va[k, 0], va[k, 1], halo_a, z, k, 0, -couple(z, k))
            adj[k, 0] = a_r
            adj[k, 1] = a_i
            return carry

        lax.fori_loop(0, NF, body, 0)

    def force(z):
        def body(k, totals):
            ang = wide(angb[k])
            inv = wide(BASE_FREQ / angb[k])
            s_r, s_i, r_r, r_i = (sr[z, k, j] for j in range(4))
            half = FORCING * img[z]
            a_r = adj[k, 0] + half * s_r
            a_i = adj[k, 1] + half * s_i
            if z + 1 < STEPS:
                rotate_a(z + 1, k, a_r, a_i)
                a_outer(z + 1, k).start()
                a_inner(z + 1, k).start()
            else:
                adj[k, 0] = a_r
                adj[k, 1] = a_i
            grad[z, 0] = jnp.where(k == 0, 0.0, grad[z, 0]) + ang * (s_r * a_i - s_i * a_r)
            grad[z, 1] = jnp.where(k == 0, 0.0, grad[z, 1]) + ang * (r_r * a_i - r_i * a_r)
            grad[z, 2] = jnp.where(k == 0, 0.0, grad[z, 2]) + inv * (s_r * a_r + s_i * a_i)
            return totals

        lax.fori_loop(0, NF, body, 0)

    trig(0)
    for copy in own_fields[:2]:
        copy.wait()
    for copy in fields[:2]:
        copy.wait_recv()
    lax.fori_loop(0, NF, first_sr, 0)
    for core in range(2):
        edge_copy(0, 0, core, sib).wait_recv()
    for k in range(SLABS):
        slow_copy(0, k, sib).wait_recv()
    first_edges()
    trig(1)

    def uses(chip):
        at = []
        for j in range(2):
            step = 0
            for z in range(1, STEPS):
                step = jnp.where(slabs[z] == 2 * chip + j, z, step)
            at.append(step)
        return jnp.minimum(at[0], at[1]), jnp.maximum(at[0], at[1]), at[0] < at[1]

    far_uses = uses(1 - chip)
    my_uses = uses(chip)
    copies = []
    arrivals = []
    gradients = []

    def finish(z, image):
        pass_a(z)
        image.wait_recv()
        img[z] = (ipart[z] + irecv[z]) * (1.0 / (2 * NF))
        force(z)
        if z >= STEPS - 2:
            n = z - (STEPS - 2)
            for j in range(3):
                gsend[n, j] = grad[far_uses[n], j]
                gradients.append(remote_copy(gsend.at[n, j], grecv.at[n, j], far))
        if z + 1 == STEPS:
            arrivals.append(remote_copy(adj.at[their_slots], adj_out.at[:, :, mine], sib))
            copies.append(local_copy(adj.at[my_slots], adj_out.at[:, :, mine]))
        copies.append(local_copy(img.at[z], img_out.at[z, mine]))
        arrivals.append(remote_copy(img.at[z], img_out.at[z, mine], sib))
    images = []
    for z in range(STEPS):
        pass_sr(z)
        images.append(remote_copy(ipart.at[z], irecv.at[z], far))
        if z == 0:
            own_fields[2].wait()
            fields[2].wait_recv()
            lax.fori_loop(0, NF, first_a, 0)
        if z == 0:
            for core in range(2):
                edge_a_copy(0, core, sib).wait_recv()
                edge_copy(0, 1, core, sib).wait_recv()
            second_edges()
        if z == 1:
            adjoint_edges()
        if z + 2 < STEPS:
            trig(z + 2)
        if LAG == 0:
            finish(z, images[z])
        elif z > 0:
            finish(z - 1, images[z - 1])
    if LAG:
        finish(STEPS - 1, images[STEPS - 1])
    sends += images
    sends += gradients

    first_is_zero = my_uses[2].astype(jnp.int32)
    own_is = jnp.where(c == 0, 1 - first_is_zero, first_is_zero)
    for j in range(3):
        for n in range(2):
            gradients[3 * n + j].wait_recv()
            gfin[n, j] = (grad[my_uses[n], j] + grecv[n, j]) * (1.0 / (2 * NF))
        gsib[j] = gfin[1 - own_is, j]
        arrivals.append(remote_copy(gsib.at[j], grad_out.at[0, j, mine], sib))
        gown[j] = gfin[own_is, j]
        copies.append(local_copy(gown.at[j], grad_out.at[0, j, mine]))
    for copy in arrivals:
        copy.wait_recv()
    for copy in copies:
        copy.wait()
    for copy in sends + arrivals:
        copy.wait_send()
    for z in range(STEPS):
        for k in range(NF):
            if z > 1:
                sr_outer(z, k).wait_send()
            sr_inner(z, k).wait_send()
            if z > 0:
                a_outer(z, k).wait_send()
            a_inner(z, k).wait_send()


def hand_over(*refs):
    copies = [
        pltpu.make_async_copy(refs[k], refs[3 + k], refs[6].at[k]) for k in range(3)
    ]
    for copy in copies:
        copy.start()
    for copy in copies:
        copy.wait()


def solution(mesh):
    bands = mesh.shape["xband"]

    def step(*args):
        args = [pltpu.with_memory_space_constraint(x, pltpu.HBM) for x in args]
        ni = args[0].shape[-1]
        half = (ROWS, ni)
        f32 = jnp.float32

        def vmem(*shape):
            return pltpu.VMEM(shape, f32)

        scratch = [
            vmem(3, 2 * ROWS, ni),
            vmem(SLABS, 2, *half),
            vmem(2, *half),
            vmem(NF, 8, 128),
            vmem(3, NF, 2, *half),
            vmem(STEPS, NF, 4, *half),
            vmem(NF, 4, *half),
            vmem(NF, 2, *half),
            vmem(NF, 2, *half),
            vmem(STEPS, NF, 2, *half),
            vmem(STEPS, 2, NF, 4, ni),
            vmem(STEPS, 2, NF, 4, ni),
            vmem(STEPS, 2, NF, 2, ni),
            vmem(STEPS, 2, NF, 2, ni),
            vmem(STEPS, *half),
            vmem(STEPS, *half),
            vmem(STEPS, *half),
            vmem(STEPS, 3, *half),
            vmem(2, 3, *half),
            vmem(2, 3, *half),
            vmem(2, 3, *half),
            vmem(3, *half),
            vmem(3, *half),
            pltpu.SMEM(args[6].shape, jnp.int32),
            pltpu.SMEM(args[7].shape, jnp.int32),
            vmem(3, 2, 2, 2 * ROWS, ni),
            vmem(2, 2, 2, 4, ni),
            vmem(2, 2, 2, 4, ni),
            vmem(2, 2, 2, ni),
            vmem(2, 2, 2, ni),
            vmem(3, 2, 8, ni),
            vmem(2, 8, ni),
            vmem(2, 3, 1, ni),
            vmem(SLABS, 3, 1, ni),
            pltpu.SemaphoreType.DMA((24,)),
            pltpu.SemaphoreType.DMA((40,)),
            pltpu.SemaphoreType.DMA((40,)),
            pltpu.SemaphoreType.DMA((STEPS, NF, 2)),
            pltpu.SemaphoreType.DMA((STEPS, NF, 2)),
            pltpu.SemaphoreType.DMA((STEPS, NF, 2)),
            pltpu.SemaphoreType.DMA((STEPS, NF, 2)),
            pltpu.SemaphoreType.DMA((2, 2)),
            pltpu.SemaphoreType.DMA((2, 2)),
            pltpu.SemaphoreType.DMA((2,)),
            pltpu.SemaphoreType.DMA((2,)),
            pltpu.SemaphoreType.DMA((4,)),
            pltpu.SemaphoreType.DMA((SLABS,)),
        ]
        any_spec = pl.BlockSpec(memory_space=pl.ANY)
        hbm_spec = pl.BlockSpec(memory_space=pltpu.HBM)
        outs = pl.pallas_call(
            functools.partial(kernel, bands),
            out_shape=(
                jax.ShapeDtypeStruct(args[2].shape, f32),
                jax.ShapeDtypeStruct((STEPS,) + args[3].shape[1:], f32),
                jax.ShapeDtypeStruct((1, 3) + args[3].shape[1:], f32),
            ),
            in_specs=[hbm_spec] * 8,
            out_specs=(any_spec,) * 3,
            scratch_shapes=scratch,
            compiler_params=pltpu.CompilerParams(
                collective_id=0, has_side_effects=True, vmem_limit_bytes=40 * 2**20
            ),
        )(*args)
        return pl.pallas_call(
            hand_over,
            out_shape=tuple(jax.ShapeDtypeStruct(x.shape, f32) for x in outs),
            in_specs=[any_spec] * 3,
            out_specs=(any_spec,) * 3,
            scratch_shapes=[pltpu.SemaphoreType.DMA((3,))],
            compiler_params=pltpu.CompilerParams(vmem_limit_bytes=4 * 2**20),
        )(*outs)

    return jax.shard_map(
        step,
        mesh=mesh,
        in_specs=(
            P("freq", None, "xband", None),
            P("freq", None, "xband", None),
            P("freq", None, "xband", None),
            P("freq", "xband", None),
            P("freq", "xband", None),
            P("freq", "xband", None),
            P(),
            P("freq"),
        ),
        out_specs=(
            P("freq", None, "xband", None),
            P(None, "xband", None),
            P("freq", None, "xband", None),
        ),
        check_vma=False,
    )
```
